128 devices in a mesh: dp: 32 (over z, x_hi, y), tensor: 4 (over x_lo, core).
Axes of the slice: x: 4 (x_hi: 2, x_lo: 2; x = x_hi * 2 + x_lo), y: 4, z: 4, core: 2. Of those that a mesh axis runs over, the one named last changes fastest.
Arguments:
- residual: bfloat16 [3, 2048, 8192], P(None, 'dp', 'tensor'), may hold values from -6 to 6
- partials: bfloat16 [3, 2048, 4, 8192], P(None, 'dp', 'tensor'), may hold values from -6 to 6
- join_weight: bfloat16 [3, 8192, 8192], P(None, 'tensor', 'dp'), may hold values from -2 to 2
- head_weight: bfloat16 [8192, 30720], P(None, 'dp'), may hold values from -4 to 4
- target_ids: int32 [3, 2048], P(None, 'tensor'), may hold values from 0 to 30719
Outputs:
- losses: float32 [3, 2048], P(None, 'tensor')
The draws below stay inside these ranges and needn't reach their ends.
All inputs are finite; a program needn't handle non-finite values.
Results may differ from the reference program's by a relative error of at most 0.0059.
Values may be sent and summed in bfloat16 or wider, within the bound.
A program may use at most 128 MiB of HBM per device.

```python
import jax
import jax.numpy as jnp
from jax import lax

D = 8192
VOCAB = 30720
TAPS = 3
UNROLL = 3
TOKENS = 2048
SPLITS = 4


def draw_join_weight(key, part):
    key = jax.random.fold_in(key, 11)
    first, second = jax.random.split(key)
    column_index = jnp.arange(D).astype(jnp.float32)
    column_scale = 3.0 ** (column_index / D) * jnp.exp(jax.random.uniform(second, (D,), jnp.float32, -0.5, 0.5))
    entries = jnp.clip(jax.random.normal(first, (TAPS, D, D), jnp.float32), -4.0, 4.0)
    return (entries * column_scale * (3.0 * D) ** (-0.5)).astype(jnp.bfloat16)


def draw_head_weight(key, part):
    key = jax.random.fold_in(key, 23)
    first, second = jax.random.split(key)
    column_index = jnp.arange(VOCAB).astype(jnp.float32)
    column_scale = 2.0 * 3.0 ** (column_index / VOCAB) * jnp.exp(jax.random.uniform(second, (VOCAB,), jnp.float32, -0.3, 0.3))
    entries = jnp.clip(jax.random.normal(first, (D, VOCAB), jnp.float32), -4.0, 4.0)
    return (entries * column_scale * D ** (-0.5)).astype(jnp.bfloat16)


def plant(values, own_key, least, high):
    dims = values.shape
    spot = [jax.random.randint(jax.random.fold_in(own_key, axis), (), 0, dims[axis]) for axis in range(len(dims))]
    values = values.at[tuple(spot)].set(least)
    longest = dims.index(max(dims))
    spot[longest] = (spot[longest] + 1) % dims[longest]
    return values.at[tuple(spot)].set(high)


def level_of(rng, dims, shards, least, high):
    level = 1.0
    for position, shards_of in shards:
        draws = jax.random.uniform(jax.random.fold_in(jax.random.fold_in(rng, 6), position), (shards_of,), jnp.float32, least / len(shards), high / len(shards))
        level = level * jnp.repeat(jnp.exp(draws), dims[position] // shards_of).reshape((-1,) + (1,) * (len(dims) - 1 - position))
    return level


def bell_draw(own_key, dims, scale, reach, cuts=(), held_as=jnp.bfloat16):
    values = scale * jax.random.normal(own_key, dims, jnp.float32)
    if cuts:
        values = values * level_of(own_key, dims, cuts, -0.22, 0.18)
    return jnp.clip(values, -reach, reach).astype(held_as)


def setup_inputs(seed: int = 0) -> dict:
    keys = jax.random.split(jax.random.key(seed), 6)
    residual = bell_draw(keys[0], (TAPS, TOKENS, D), 1.0, 6.0, ((1, 32), (2, 4)))
    partials = bell_draw(keys[1], (TAPS, TOKENS, SPLITS, D), 1.0, 6.0, ((1, 32), (2, 4)))
    join_weight = draw_join_weight(jax.random.fold_in(keys[5], 71), 0)
    head_weight = draw_head_weight(jax.random.fold_in(keys[5], 71), 0)
    target_ids = plant(jax.random.randint(keys[4], (UNROLL, TOKENS), 0, VOCAB), jax.random.fold_in(keys[4], 1), 0, VOCAB - 1).astype(jnp.int32)
    return dict(residual=residual, partials=partials, join_weight=join_weight, head_weight=head_weight, target_ids=target_ids)


def reference(residual, partials, join_weight, head_weight, target_ids):
    tap_states = (residual.astype(jnp.float32) + lax.optimization_barrier(jnp.sum(partials.astype(jnp.float32), axis=2))).astype(jnp.bfloat16)
    joined_rows = jnp.zeros((TOKENS, D), jnp.float32)
    for layer in range(TAPS):
        joined_rows = joined_rows + jnp.dot(tap_states[layer], join_weight[layer], preferred_element_type=jnp.float32)
    root_mean = jnp.sqrt(lax.optimization_barrier(jnp.mean(joined_rows * joined_rows, axis=1, keepdims=True)) + 1e-05)
    normed = (joined_rows / root_mean).astype(jnp.bfloat16)
    logits = jnp.dot(normed, head_weight, preferred_element_type=jnp.float32)
    log_total = jnp.log(lax.optimization_barrier(jnp.sum(jnp.exp(logits), axis=1)))
    picked = jnp.take_along_axis(logits, target_ids.T.astype(jnp.int32), axis=1).T
    return log_total[None, :] - picked
```

```python
import jax
import jax.numpy as jnp
from jax import lax
from jax.experimental import pallas as pl
from jax.experimental.pallas import tpu as pltpu
from jax.sharding import PartitionSpec as P

D = 8192
EPS = 1e-05
F32 = jnp.float32
BF16 = jnp.bfloat16
COPIES = 160


def kernel(
    residual,
    partial,
    weight,
    head,
    ids,
    losses,
    part_v,
    res_v,
    sib_in,
    pair_out,
    pair_in,
    tap_out,
    taps,
    wz,
    head_v,
    acc,
    c_out,
    c_in,
    x_out,
    x_in,
    z_out,
    z_in,
    z_own,
    joined,
    logits,
    squares,
    stat_a,
    stat_b,
    send_sem,
    recv_sem,
    local_sem,
):
    dp = lax.axis_index("dp")
    t = lax.axis_index("tensor")
    z, xh, y = dp // 8, lax.rem(dp // 4, 2), lax.rem(dp, 4)
    xl, c = t // 2, lax.rem(t, 2)

    def device(zz, hh, yy, ll, cc):
        return (zz * 8 + hh * 4 + yy, ll * 2 + cc)

    def zo(d):
        return lax.rem(z + d, 4)

    def yo(d):
        return lax.rem(y + d, 4)

    sibling = device(z, xh, y, xl, 1 - c)
    pair = device(z, xh, y, 1 - xl, c)
    across = device(z, 1 - xh, y, xl, c)
    y_peer = [None] + [device(z, xh, yo(d), xl, c) for d in (1, 2, 3)]
    z_peer = [None] + [device(zo(d), xh, y, xl, c) for d in (1, 2, 3)]
    far_peer = [across] + [device(z, 1 - xh, yo(d), xl, c) for d in (1, 2, 3)]

    barrier = pltpu.get_barrier_semaphore()
    peers = [sibling, pair] + y_peer[1:] + z_peer[1:] + far_peer
    for peer in peers:
        pl.semaphore_signal(barrier, inc=1, device_id=peer, device_id_type=pl.DeviceIdType.MESH)

    local = []

    def fetch(src, dst):
        copy = pltpu.make_async_copy(src, dst, local_sem.at[len(local)])
        copy.start()
        local.append(copy)
        return copy

    part_copy = [fetch(partial.at[k], part_v.at[k]) for k in range(3)]
    res_copy = fetch(residual, res_v)
    wz_copy = fetch(weight.at[:, pl.ds(pl.multiple_of(z * 512, 512), 512), :], wz.at[:, z])
    pl.semaphore_wait(barrier, len(peers))

    sent = []

    def make(src, dst, number, peer):
        return pltpu.make_async_remote_copy(
            src_ref=src,
            dst_ref=dst,
            send_sem=send_sem.at[number],
            recv_sem=recv_sem.at[number],
            device_id=peer,
            device_id_type=pl.DeviceIdType.MESH,
        )

    counter = iter(range(COPIES))

    def send(src, dst, peer, number=None):
        number = next(counter) if number is None else number
        copy = make(src, dst, number, peer)
        copy.start()
        sent.append(copy)
        return number

    def arrive(dst, number, peer):
        make(dst, dst, number, peer).wait_recv()

    sib_n = []
    for k in range(3):
        row = []
        for l in range(2):
            cols = pl.ds(pl.multiple_of((l * 2 + 1 - c) * 2048, 2048), 2048)
            row.append(send(partial.at[k, :, cols], sib_in.at[k, l], sibling))
        sib_n.append(row)
    wz_n = [None]
    for d in (1, 2, 3):
        rows = pl.ds(pl.multiple_of(zo(d) * 512, 512), 512)
        wz_n.append(send(weight.at[:, rows, :], wz.at[:, z], z_peer[d]))
    head_copy = fetch(head, head_v)

    own_cols = pl.ds(pl.multiple_of(t * 2048, 2048), 2048)
    pair_cols = pl.ds(pl.multiple_of(((1 - xl) * 2 + c) * 2048, 2048), 2048)
    pair_n = []
    for k in range(3):
        part_copy[k].wait()
        arrive(sib_in.at[k, 0], sib_n[k][0], sibling)
        arrive(sib_in.at[k, 1], sib_n[k][1], sibling)
        pair_out[k] = (part_v[k, :, pair_cols].astype(F32) + sib_in[k, 1 - xl].astype(F32)).astype(BF16)
        pair_n.append(send(pair_out.at[k], pair_in.at[k], pair))
    res_copy.wait()
    tap_n = []
    for k in range(3):
        arrive(pair_in.at[k], pair_n[k], pair)
        tap = (
            res_v[k].astype(F32)
            + (part_v[k, :, own_cols].astype(F32) + sib_in[k, xl].astype(F32))
            + pair_in[k].astype(F32)
        ).astype(BF16)
        for q in range(4):
            tap_out[k, q] = tap[:, q * 512 : (q + 1) * 512]
        row = [None]
        for d in (1, 2, 3):
            row.append(send(tap_out.at[k, zo(d)], taps.at[k, y, xh, z], z_peer[d]))
        tap_n.append(row)
        taps[k, y, xh, z] = tap_out[k, z]

    far_n = []
    ring_n = {}
    for k in range(3):
        for d in (1, 2, 3):
            arrive(taps.at[k, y, xh, zo(4 - d)], tap_n[k][d], z_peer[4 - d])
        block = taps.at[k, y, xh]
        far_n.append(send(block, block, across))
        ring_n[k, 0] = [send(block, block, y_peer[1]), send(block, block, y_peer[3])]
    for k in range(3):
        arrive(taps.at[k, y, 1 - xh], far_n[k], across)
        block = taps.at[k, y, 1 - xh]
        ring_n[k, 1] = [send(block, block, y_peer[1]), send(block, block, y_peer[3])]

    chunk_y = [y, yo(3), yo(1), yo(2)]
    c_n, x_n, z_n = {}, {}, {}

    def multiply(j):
        slot = j % 2
        row = chunk_y[j]

        @pl.loop(0, 4)
        def _(q):
            total = jnp.zeros((512, 256), F32)
            for k in range(3):
                total += jnp.dot(taps[k, row].reshape(512, 512), wz[k, q], preferred_element_type=F32)
            acc[slot, q] = total.reshape(2, 4, 64, 256)
            for l in range(2):
                c_out[j, q, :, l] = acc[slot, q, :, l * 2 + 1 - c].astype(BF16)

        c_n[j] = send(c_out.at[j], c_in.at[j], sibling)

    def over_core(j):
        slot = j % 2
        arrive(c_in.at[j], c_n[j], sibling)

        @pl.loop(0, 4)
        def _(q):
            x_out[j, q] = (acc[slot, q, :, (1 - xl) * 2 + c] + c_in[j, q, :, 1 - xl].astype(F32)).astype(BF16)

        x_n[j] = send(x_out.at[j], x_in.at[j], pair)

    def over_pair(j):
        slot = j % 2
        arrive(x_in.at[j], x_n[j], pair)

        def value(q):
            return acc[slot, q, :, t] + c_in[j, q, :, xl].astype(F32) + x_in[j, q].astype(F32)

        @pl.loop(0, 4)
        def _(q):
            z_out[j, q] = value(q).astype(BF16)

        z_n[j] = [None] + [send(z_out.at[j, zo(d)], z_in.at[j, d - 1], z_peer[d]) for d in (1, 2, 3)]
        z_own[j] = value(z)

    def over_z(j):
        total = z_own[j]
        for d in (1, 2, 3):
            arrive(z_in.at[j, d - 1], z_n[j][d], z_peer[4 - d])
            total = total + z_in[j, d - 1].astype(F32)
        joined[z, xh, y, :, chunk_y[j]] = total.astype(BF16)

    half_n = {}

    def pass_on(h):
        hh = xh if h == 0 else 1 - xh
        for k in range(3):
            arrive(taps.at[k, yo(3), hh], ring_n[k, h][0], y_peer[3])
            low = taps.at[k, yo(3), hh, pl.ds(0, 2)]
            first = send(low, low, y_peer[1])
            arrive(taps.at[k, yo(1), hh], ring_n[k, h][1], y_peer[1])
            high = taps.at[k, yo(1), hh, pl.ds(2, 2)]
            half_n[k, h] = [first, send(high, high, y_peer[3])]

    wz_copy.wait()
    for d in (1, 2, 3):
        arrive(wz.at[:, zo(4 - d)], wz_n[d], z_peer[4 - d])
    multiply(0)
    pass_on(0)
    over_core(0)
    pass_on(1)
    multiply(1)
    over_pair(0)
    over_core(1)
    multiply(2)
    over_z(0)
    over_pair(1)
    over_core(2)
    for h in range(2):
        hh = xh if h == 0 else 1 - xh
        for k in range(3):
            arrive(taps.at[k, yo(2), hh, pl.ds(0, 2)], half_n[k, h][0], y_peer[3])
            arrive(taps.at[k, yo(2), hh, pl.ds(2, 2)], half_n[k, h][1], y_peer[1])
    multiply(3)
    over_z(1)
    over_pair(2)
    over_core(3)
    over_z(2)
    over_pair(3)
    over_z(3)

    logits[...] = jnp.zeros_like(logits)
    squares[...] = jnp.zeros_like(squares)
    mine = joined.at[z, xh, y]
    g_far = send(mine, mine, across)
    g_ring = {}
    for s in range(2):
        if s == 1:
            arrive(joined.at[z, 1 - xh, y], g_far, across)
        ss = xh if s == 0 else 1 - xh
        block = joined.at[z, ss, y, 0]
        g_ring[0, s] = [send(block, block, y_peer[1]), send(block, block, y_peer[3])]
        block = joined.at[z, ss, y, 1]
        g_ring[1, s] = [send(block, block, z_peer[1]), send(block, block, z_peer[3])]

    def place(h, a, b, ss=None, part=None):
        zz, yy = (zo(b), yo(a)) if h == 0 else (zo(a), yo(b))
        sl = slice(None) if ss is None else ss
        if part is None:
            return joined.at[zz, sl, yy, h]
        return joined.at[zz, sl, yy, h, pl.ds(part * 2, 2)]

    one = [y_peer, z_peer]
    two = [z_peer, y_peer]
    g_two = {}

    def start_two(h, a):
        block = place(h, a, 0)
        g_two[h, a] = [send(block, block, two[h][1]), send(block, block, two[h][3])]

    for h in range(2):
        start_two(h, 0)
    g_half = {}
    for s in range(2):
        ss = xh if s == 0 else 1 - xh
        for h in range(2):
            arrive(place(h, 3, 0, ss), g_ring[h, s][0], one[h][3])
            low = place(h, 3, 0, ss, 0)
            first = send(low, low, one[h][1])
            arrive(place(h, 1, 0, ss), g_ring[h, s][1], one[h][1])
            high = place(h, 1, 0, ss, 1)
            g_half[h, s] = [first, send(high, high, one[h][3])]
    for h in range(2):
        start_two(h, 3)
        start_two(h, 1)
    head_copy.wait()

    def score(h, b):
        @pl.loop(0, 8)
        def _(i):
            if h == 0:
                zz, ss, yy = zo(b), i // 4, lax.rem(i, 4)
            else:
                zz, ss, yy = i // 2, lax.rem(i, 2), yo(b)
            block = joined[zz, ss, yy, h].reshape(256, 256)
            rows = pl.ds(pl.multiple_of(((zz * 2 + ss) * 4 + yy) * 256, 256), 256)
            logits[h] += lax.dot_general(
                block, head_v[:, rows], (((1,), (1,)), ((), ())), preferred_element_type=F32
            )
            wide = block.astype(F32)
            left, right = wide[:, :128], wide[:, 128:]
            squares[h] += left * left + right * right

    g_last = {}

    def forward_two(h, a):
        arrive(place(h, a, 3), g_two[h, a][0], two[h][3])
        low = place(h, a, 3, None, 0)
        first = send(low, low, two[h][1])
        arrive(place(h, a, 1), g_two[h, a][1], two[h][1])
        high = place(h, a, 1, None, 1)
        g_last[h, a] = [first, send(high, high, two[h][3])]

    for h in range(2):
        forward_two(h, 0)
    for h in range(2):
        for s in range(2):
            ss = xh if s == 0 else 1 - xh
            arrive(place(h, 2, 0, ss, 0), g_half[h, s][0], one[h][3])
            arrive(place(h, 2, 0, ss, 1), g_half[h, s][1], one[h][1])
        start_two(h, 2)
    for h in range(2):
        score(h, 0)
    for a in (3, 1, 2):
        for h in range(2):
            forward_two(h, a)
    for h in range(2):
        score(h, 1)
        score(h, 3)
    for h in range(2):
        for a in (0, 3, 1, 2):
            arrive(place(h, a, 2, None, 0), g_last[h, a][0], two[h][3])
            arrive(place(h, a, 2, None, 1), g_last[h, a][1], two[h][1])
        score(h, 2)

    offset = dp * 960
    lane = lax.broadcasted_iota(jnp.int32, (256, 128), 1)
    for h in range(2):
        mean = jnp.sum(squares[h], axis=1, keepdims=True) / D
        scaled = logits[h] / jnp.sqrt(mean + EPS)
        column = lax.broadcasted_iota(jnp.int32, (256, 960), 1) + offset
        stats = jnp.where(lane == 0, jnp.sum(jnp.exp(scaled), axis=1, keepdims=True), 0.0)
        for s in range(3):
            wanted = ids[h * 256 : (h + 1) * 256, s : s + 1]
            picked = jnp.sum(jnp.where(column == wanted, scaled, 0.0), axis=1, keepdims=True)
            stats = jnp.where(lane == s + 1, picked, stats)
        stat_a[0, :, h * 256 : (h + 1) * 256] = stats.T[:8]
    a_n = [None] + [send(stat_a.at[0], stat_a.at[d], z_peer[d]) for d in (1, 2, 3)]
    total = stat_a[0]
    for d in (1, 2, 3):
        arrive(stat_a.at[d], a_n[d], z_peer[4 - d])
        total = total + stat_a[d]
    stat_b[0, 0] = total
    b_n = {}
    for s in range(2):
        for d in range(4):
            if s or d:
                peer = far_peer[d] if s else y_peer[d]
                b_n[s, d] = send(stat_b.at[0, 0], stat_b.at[s, d], peer)
    for s in range(2):
        for d in range(4):
            if s or d:
                peer = far_peer[(4 - d) % 4] if s else y_peer[4 - d]
                arrive(stat_b.at[s, d], b_n[s, d], peer)
                total = total + stat_b[s, d]
    losses[...] = jnp.log(total[0:1]) - total[1:4]
    for copy in sent:
        copy.wait_send()


def shards(residual, partials, join_weight, head_weight, target_ids):
    vmem = pl.BlockSpec(memory_space=pltpu.VMEM)
    hbm = pl.BlockSpec(memory_space=pl.ANY)
    return pl.pallas_call(
        kernel,
        out_shape=jax.ShapeDtypeStruct((3, 512), F32),
        in_specs=[hbm, hbm, hbm, hbm, vmem],
        out_specs=vmem,
        scratch_shapes=[
            pltpu.VMEM((3, 64, 8192), BF16),
            pltpu.VMEM((3, 64, 2048), BF16),
            pltpu.VMEM((3, 2, 64, 2048), BF16),
            pltpu.VMEM((3, 64, 2048), BF16),
            pltpu.VMEM((3, 64, 2048), BF16),
            pltpu.VMEM((3, 4, 64, 512), BF16),
            pltpu.VMEM((3, 4, 2, 4, 64, 512), BF16),
            pltpu.VMEM((3, 4, 512, 256), BF16),
            pltpu.VMEM((960, 8192), BF16),
            pltpu.VMEM((2, 4, 2, 4, 64, 256), F32),
            pltpu.VMEM((4, 4, 2, 2, 64, 256), BF16),
            pltpu.VMEM((4, 4, 2, 2, 64, 256), BF16),
            pltpu.VMEM((4, 4, 2, 64, 256), BF16),
            pltpu.VMEM((4, 4, 2, 64, 256), BF16),
            pltpu.VMEM((4, 4, 2, 64, 256), BF16),
            pltpu.VMEM((4, 3, 2, 64, 256), BF16),
            pltpu.VMEM((4, 2, 64, 256), F32),
            pltpu.VMEM((4, 2, 4, 2, 4, 64, 256), BF16),
            pltpu.VMEM((2, 256, 960), F32),
            pltpu.VMEM((2, 256, 128), F32),
            pltpu.VMEM((4, 8, 512), F32),
            pltpu.VMEM((2, 4, 8, 512), F32),
            pltpu.SemaphoreType.DMA((COPIES,)),
            pltpu.SemaphoreType.DMA((COPIES,)),
            pltpu.SemaphoreType.DMA((8,)),
        ],
        compiler_params=pltpu.CompilerParams(
            collective_id=0, has_side_effects=True, vmem_limit_bytes=63 * 1024 * 1024
        ),
    )(residual, partials.reshape(3, 64, 8192), join_weight, head_weight.T, target_ids.T)


def solution(mesh):
    placed = (
        P(None, "dp", "tensor"),
        P(None, "dp", "tensor", None),
        P(None, "tensor", "dp"),
        P(None, "dp"),
        P(None, "tensor"),
    )
    return jax.shard_map(
        shards, mesh=mesh, in_specs=placed, out_specs=P(None, "tensor"), check_vma=False
    )
```

```python
import jax
import jax.numpy as jnp
from jax import lax
from jax.experimental import pallas as pl
from jax.experimental.pallas import tpu as pltpu
from jax.sharding import PartitionSpec as P

D = 8192
EPS = 1e-05
F32 = jnp.float32
BF16 = jnp.bfloat16
COPIES = 280


def kernel(
    residual,
    partial,
    weight,
    head,
    ids,
    losses,
    part_v,
    res_v,
    sib_in,
    pair_out,
    pair_in,
    tap_out,
    taps,
    wz,
    head_v,
    acc,
    c_out,
    c_in,
    r_out,
    r_in,
    r_own,
    joined,
    logits,
    squares,
    stat_a,
    stat_b,
    send_sem,
    recv_sem,
    local_sem,
):
    dp = lax.axis_index("dp")
    t = lax.axis_index("tensor")
    z, xh, y = dp // 8, lax.rem(dp // 4, 2), lax.rem(dp, 4)
    xl, c = t // 2, lax.rem(t, 2)

    def device(zz, hh, yy, ll, cc):
        return (zz * 8 + hh * 4 + yy, ll * 2 + cc)

    def zo(d):
        return lax.rem(z + d, 4)

    def yo(d):
        return lax.rem(y + d, 4)

    sibling = device(z, xh, y, xl, 1 - c)
    pair = device(z, xh, y, 1 - xl, c)
    across = device(z, 1 - xh, y, xl, c)
    y_peer = [None] + [device(z, xh, yo(d), xl, c) for d in (1, 2, 3)]
    z_peer = [None] + [device(zo(d), xh, y, xl, c) for d in (1, 2, 3)]
    far_peer = [across] + [device(z, 1 - xh, yo(d), xl, c) for d in (1, 2, 3)]

    barrier = pltpu.get_barrier_semaphore()
    pair_z_peer = [pair] + [device(zo(d), xh, y, 1 - xl, c) for d in (1, 2, 3)]
    peers = [sibling] + y_peer[1:] + z_peer[1:] + far_peer + pair_z_peer
    for peer in peers:
        pl.semaphore_signal(barrier, inc=1, device_id=peer, device_id_type=pl.DeviceIdType.MESH)

    local = []

    def fetch(src, dst):
        copy = pltpu.make_async_copy(src, dst, local_sem.at[len(local)])
        copy.start()
        local.append(copy)
        return copy

    part_copy = [fetch(partial.at[k], part_v.at[k]) for k in range(3)]
    res_copy = fetch(residual, res_v)
    wz_copy = fetch(weight.at[:, pl.ds(pl.multiple_of(z * 512, 512), 512), :], wz.at[:, z])
    pl.semaphore_wait(barrier, len(peers))

    sent = []

    def make(src, dst, number, peer):
        return pltpu.make_async_remote_copy(
            src_ref=src,
            dst_ref=dst,
            send_sem=send_sem.at[number],
            recv_sem=recv_sem.at[number],
            device_id=peer,
            device_id_type=pl.DeviceIdType.MESH,
        )

    counter = iter(range(COPIES))

    def send(src, dst, peer, number=None):
        number = next(counter) if number is None else number
        copy = make(src, dst, number, peer)
        copy.start()
        sent.append(copy)
        return number

    def arrive(dst, number, peer):
        make(dst, dst, number, peer).wait_recv()

    sib_n = []
    for k in range(3):
        row = []
        for l in range(2):
            cols = pl.ds(pl.multiple_of((l * 2 + 1 - c) * 2048, 2048), 2048)
            row.append(send(partial.at[k, :, cols], sib_in.at[k, l], sibling))
        sib_n.append(row)
    wz_n = {}

    def swap(first, count):
        for d in (1, 2, 3):
            rows = pl.ds(pl.multiple_of(zo(d) * 512, 512), 512)
            taps_of = pl.ds(first, count)
            wz_n[first, d] = send(weight.at[taps_of, rows, :], wz.at[taps_of, z], z_peer[d])

    swap(0, 1)
    head_copy = fetch(head, head_v)

    own_cols = pl.ds(pl.multiple_of(t * 2048, 2048), 2048)
    pair_cols = pl.ds(pl.multiple_of(((1 - xl) * 2 + c) * 2048, 2048), 2048)
    pair_n = []
    for k in range(3):
        part_copy[k].wait()
        arrive(sib_in.at[k, 0], sib_n[k][0], sibling)
        arrive(sib_in.at[k, 1], sib_n[k][1], sibling)
        pair_out[k] = (part_v[k, :, pair_cols].astype(F32) + sib_in[k, 1 - xl].astype(F32)).astype(BF16)
        pair_n.append(send(pair_out.at[k], pair_in.at[k], pair))
    res_copy.wait()
    tap_n = {}
    far_n = {}
    ring_n = {}
    half_n = {}

    def make_taps(k):
        arrive(pair_in.at[k], pair_n[k], pair)
        tap = (
            res_v[k].astype(F32)
            + (part_v[k, :, own_cols].astype(F32) + sib_in[k, xl].astype(F32))
            + pair_in[k].astype(F32)
        ).astype(BF16)
        for q in range(4):
            tap_out[k, q] = tap[:, q * 512 : (q + 1) * 512]
        for d in (1, 2, 3):
            tap_n[k, d] = send(tap_out.at[k, zo(d)], taps.at[k, y, xh, z], z_peer[d])
        taps[k, y, xh, z] = tap_out[k, z]

    def gather(k):
        for d in (1, 2, 3):
            arrive(taps.at[k, y, xh, zo(4 - d)], tap_n[k, d], z_peer[4 - d])
        block = taps.at[k, y, xh]
        far_n[k] = send(block, block, across)
        ring_n[k, 0] = [send(block, block, y_peer[1]), send(block, block, y_peer[3])]

    def gather_far(k):
        arrive(taps.at[k, y, 1 - xh], far_n[k], across)
        block = taps.at[k, y, 1 - xh]
        ring_n[k, 1] = [send(block, block, y_peer[1]), send(block, block, y_peer[3])]

    def pass_on(k, h):
        hh = 1 - xh if h else xh
        arrive(taps.at[k, yo(3), hh], ring_n[k, h][0], y_peer[3])
        low = taps.at[k, yo(3), hh, pl.ds(0, 2)]
        first = send(low, low, y_peer[1])
        arrive(taps.at[k, yo(1), hh], ring_n[k, h][1], y_peer[1])
        high = taps.at[k, yo(1), hh, pl.ds(2, 2)]
        half_n[k, h] = [first, send(high, high, y_peer[3])]

    make_taps(0)
    make_taps(1)
    gather(0)
    make_taps(2)
    swap(1, 2)
    gather(1)
    gather_far(0)
    pass_on(0, 0)
    gather(2)
    for k in (1, 2):
        gather_far(k)
        pass_on(k, 0)

    chunk_y = [y, yo(3), yo(1), yo(2)]
    c_n, r_n = {}, {}

    def multiply(j):
        slot = j % 2
        row = chunk_y[j]

        @pl.loop(0, 4)
        def _(q):
            total = jnp.zeros((512, 256), F32)
            for k in range(3):
                total += jnp.dot(taps[k, row].reshape(512, 512), wz[k, q], preferred_element_type=F32)
            acc[slot, q] = total.reshape(2, 4, 64, 256)
            for l in range(2):
                c_out[j, q, :, l] = acc[slot, q, :, l * 2 + 1 - c].astype(BF16)

        c_n[j] = send(c_out.at[j], c_in.at[j], sibling)

    ways = [(l, d) for l in range(2) for d in range(4) if l or d]

    def over_core(j):
        slot = j % 2
        arrive(c_in.at[j], c_n[j], sibling)

        @pl.loop(0, 4)
        def _(q):
            for l in range(2):
                value = acc[slot, q, :, l * 2 + c] + c_in[j, q, :, l].astype(F32)
                r_out[j, l, q] = value.astype(BF16)

        for i, (l, d) in enumerate(ways):
            peer = pair_z_peer[d] if l else z_peer[d]
            ll = 1 - xl if l else xl
            r_n[j, i] = send(r_out.at[j, ll, zo(d)], r_in.at[j, i], peer)
        r_own[j] = acc[slot, z, :, t] + c_in[j, z, :, xl].astype(F32)

    def reduce(j):
        total = r_own[j]
        for i, (l, d) in enumerate(ways):
            arrive(r_in.at[j, i], r_n[j, i], pair_z_peer[(4 - d) % 4] if l else z_peer[4 - d])
            total = total + r_in[j, i].astype(F32)
        joined[z, xh, y, j] = total.astype(BF16)

    def last_taps():
        for h in range(2):
            hh = xh if h == 0 else 1 - xh
            for k in range(3):
                arrive(taps.at[k, yo(2), hh, pl.ds(0, 2)], half_n[k, h][0], y_peer[3])
                arrive(taps.at[k, yo(2), hh, pl.ds(2, 2)], half_n[k, h][1], y_peer[1])

    group = [pl.ds(0, 1), pl.ds(1, 2), pl.ds(3, 1)]
    one = [y_peer, z_peer]
    two = [z_peer, y_peer]
    g_far, g_ring, g_half, g_two, g_last = {}, {}, {}, {}, {}

    def place(g, h, a, b, ss=None, part=None):
        zz, yy = (zo(b), yo(a)) if h == 0 else (zo(a), yo(b))
        sl = slice(None) if ss is None else ss
        rows = slice(None) if part is None else pl.ds(part * 32, 32)
        return joined.at[zz, sl, yy, group[g], h, rows]

    def start_one(g, s):
        ss = xh if s == 0 else 1 - xh
        for h in range(2):
            block = place(g, h, 0, 0, ss)
            g_ring[g, h, s] = [send(block, block, one[h][1]), send(block, block, one[h][3])]

    def start_two(g, h, a):
        block = place(g, h, a, 0)
        g_two[g, h, a] = [send(block, block, two[h][1]), send(block, block, two[h][3])]

    def p_start(g):
        mine = joined.at[z, xh, y, group[g]]
        g_far[g] = send(mine, mine, across)
        start_one(g, 0)

    def p_far(g):
        arrive(joined.at[z, 1 - xh, y, group[g]], g_far[g], across)
        start_one(g, 1)
        for h in range(2):
            start_two(g, h, 0)

    def p_one(g):
        for s in range(2):
            ss = xh if s == 0 else 1 - xh
            for h in range(2):
                arrive(place(g, h, 3, 0, ss), g_ring[g, h, s][0], one[h][3])
                low = place(g, h, 3, 0, ss, 0)
                first = send(low, low, one[h][1])
                arrive(place(g, h, 1, 0, ss), g_ring[g, h, s][1], one[h][1])
                high = place(g, h, 1, 0, ss, 1)
                g_half[g, h, s] = [first, send(high, high, one[h][3])]
        for h in range(2):
            start_two(g, h, 3)
            start_two(g, h, 1)

    def p_one_far(g):
        for h in range(2):
            for s in range(2):
                ss = xh if s == 0 else 1 - xh
                arrive(place(g, h, 2, 0, ss, 0), g_half[g, h, s][0], one[h][3])
                arrive(place(g, h, 2, 0, ss, 1), g_half[g, h, s][1], one[h][1])
            start_two(g, h, 2)

    def p_two(g, a):
        for h in range(2):
            arrive(place(g, h, a, 3), g_two[g, h, a][0], two[h][3])
            low = place(g, h, a, 3, None, 0)
            first = send(low, low, two[h][1])
            arrive(place(g, h, a, 1), g_two[g, h, a][1], two[h][1])
            high = place(g, h, a, 1, None, 1)
            g_last[g, h, a] = [first, send(high, high, two[h][3])]

    def p_end(g):
        for h in range(2):
            for a in (0, 3, 1, 2):
                arrive(place(g, h, a, 2, None, 0), g_last[g, h, a][0], two[h][3])
                arrive(place(g, h, a, 2, None, 1), g_last[g, h, a][1], two[h][1])

    offsets = (0, 3, 1, 2)
    chunks = [(0,), (1, 2), (3,)]

    def score(g, first, count):
        n = len(chunks[g])

        @pl.loop(first, first + count)
        def _(yy):
            product = jnp.zeros((960, n * 128), F32)
            square = jnp.zeros((n * 128, 128), F32)
            for i in range(8):
                block = joined[i // 2, i % 2, yy, group[g]].reshape(n * 128, 256)
                cols = pl.ds(pl.multiple_of((i * 4 + yy) * 256, 256), 256)
                product += lax.dot_general(
                    head_v[:, cols], block, (((1,), (1,)), ((), ())), preferred_element_type=F32
                )
                wide = block.astype(F32)
                left, right = wide[:, :128], wide[:, 128:]
                square += left * left + right * right
            for p, j in enumerate(chunks[g]):
                row = lax.rem(yy + offsets[j], 4)
                logits[row] += product[:, p * 128 : (p + 1) * 128]
                squares[row] += square[p * 128 : (p + 1) * 128]

    logits[...] = jnp.zeros_like(logits)
    squares[...] = jnp.zeros_like(squares)
    wz_copy.wait()
    for d in (1, 2, 3):
        for first, count in ((0, 1), (1, 2)):
            arrive(wz.at[pl.ds(first, count), zo(4 - d)], wz_n[first, d], z_peer[4 - d])
    multiply(0)
    over_core(0)
    for k in range(3):
        pass_on(k, 1)
    multiply(1)
    over_core(1)
    reduce(0)
    p_start(0)
    multiply(2)
    p_far(0)
    over_core(2)
    p_one(0)
    reduce(1)
    reduce(2)
    p_start(1)
    last_taps()
    multiply(3)
    p_far(1)
    p_one_far(0)
    p_two(0, 0)
    over_core(3)
    p_one(1)
    p_two(0, 3)
    p_two(0, 1)
    p_two(0, 2)
    reduce(3)
    p_start(2)
    p_one_far(1)
    p_two(1, 0)
    p_far(2)
    p_two(1, 3)
    p_one(2)
    p_two(1, 1)
    head_copy.wait()
    p_end(0)
    score(0, 0, 2)
    p_one_far(2)
    p_two(2, 0)
    p_two(1, 2)
    score(0, 2, 2)
    p_two(2, 3)
    p_two(2, 1)
    p_two(2, 2)
    p_end(1)
    score(1, 0, 4)
    p_end(2)
    score(2, 0, 4)

    offset = dp * 960
    column = lax.broadcasted_iota(jnp.int32, (960, 128), 0) + offset
    blank = jnp.zeros((4, 128), F32)
    for row in range(4):
        mean = jnp.sum(squares[row].T, axis=0, keepdims=True) / D
        scaled = logits[row] / jnp.sqrt(mean + EPS)
        stats = [jnp.sum(jnp.exp(scaled), axis=0, keepdims=True)]
        for s in range(3):
            wanted = ids[row, s : s + 1]
            stats.append(jnp.sum(jnp.where(column == wanted, scaled, 0.0), axis=0, keepdims=True))
        stat_a[0, :, row * 128 : (row + 1) * 128] = jnp.concatenate(stats + [blank], axis=0)
    a_n = [None] + [send(stat_a.at[0], stat_a.at[d], z_peer[d]) for d in (1, 2, 3)]
    total = stat_a[0]
    for d in (1, 2, 3):
        arrive(stat_a.at[d], a_n[d], z_peer[4 - d])
        total = total + stat_a[d]
    stat_b[0, 0] = total
    b_n = {}
    for s in range(2):
        for d in range(4):
            if s or d:
                peer = far_peer[d] if s else y_peer[d]
                b_n[s, d] = send(stat_b.at[0, 0], stat_b.at[s, d], peer)
    for s in range(2):
        for d in range(4):
            if s or d:
                peer = far_peer[(4 - d) % 4] if s else y_peer[4 - d]
                arrive(stat_b.at[s, d], b_n[s, d], peer)
                total = total + stat_b[s, d]
    losses[...] = jnp.log(total[0:1]) - total[1:4]
    for copy in sent:
        copy.wait_send()


def shards(residual, partials, join_weight, head_weight, target_ids):
    vmem = pl.BlockSpec(memory_space=pltpu.VMEM)
    hbm = pl.BlockSpec(memory_space=pl.ANY)
    ids = target_ids.reshape(3, 2, 4, 64).transpose(2, 0, 1, 3).reshape(4, 3, 128)
    result = pl.pallas_call(
        kernel,
        out_shape=jax.ShapeDtypeStruct((3, 512), F32),
        in_specs=[hbm, hbm, hbm, hbm, vmem],
        out_specs=vmem,
        scratch_shapes=[
            pltpu.VMEM((3, 64, 8192), BF16),
            pltpu.VMEM((3, 64, 2048), BF16),
            pltpu.VMEM((3, 2, 64, 2048), BF16),
            pltpu.VMEM((3, 64, 2048), BF16),
            pltpu.VMEM((3, 64, 2048), BF16),
            pltpu.VMEM((3, 4, 64, 512), BF16),
            pltpu.VMEM((3, 4, 2, 4, 64, 512), BF16),
            pltpu.VMEM((3, 4, 512, 256), BF16),
            pltpu.VMEM((960, 8192), BF16),
            pltpu.VMEM((2, 4, 2, 4, 64, 256), F32),
            pltpu.VMEM((4, 4, 2, 2, 64, 256), BF16),
            pltpu.VMEM((4, 4, 2, 2, 64, 256), BF16),
            pltpu.VMEM((4, 2, 4, 2, 64, 256), BF16),
            pltpu.VMEM((4, 7, 2, 64, 256), BF16),
            pltpu.VMEM((4, 2, 64, 256), F32),
            pltpu.VMEM((4, 2, 4, 4, 2, 64, 256), BF16),
            pltpu.VMEM((4, 960, 128), F32),
            pltpu.VMEM((4, 128, 128), F32),
            pltpu.VMEM((4, 8, 512), F32),
            pltpu.VMEM((2, 4, 8, 512), F32),
            pltpu.SemaphoreType.DMA((COPIES,)),
            pltpu.SemaphoreType.DMA((COPIES,)),
            pltpu.SemaphoreType.DMA((8,)),
        ],
        compiler_params=pltpu.CompilerParams(
            collective_id=0, has_side_effects=True, vmem_limit_bytes=63 * 1024 * 1024
        ),
    )(residual, partials.reshape(3, 64, 8192), join_weight, head_weight.T, ids)
    return result.reshape(3, 4, 2, 64).transpose(0, 2, 1, 3).reshape(3, 512)


def solution(mesh):
    placed = (
        P(None, "dp", "tensor"),
        P(None, "dp", "tensor", None),
        P(None, "tensor", "dp"),
        P(None, "dp"),
        P(None, "tensor"),
    )
    return jax.shard_map(
        shards, mesh=mesh, in_specs=placed, out_specs=P(None, "tensor"), check_vma=False
    )
```

```python
import jax
import jax.numpy as jnp
from jax import lax
from jax.experimental import pallas as pl
from jax.experimental.pallas import tpu as pltpu
from jax.sharding import PartitionSpec as P

D = 8192
EPS = 1e-05
F32 = jnp.float32
BF16 = jnp.bfloat16
COPIES = 360


def kernel(
    residual,
    partial,
    weight,
    head,
    ids,
    losses,
    part_v,
    res_v,
    sib_in,
    pair_out,
    pair_in,
    tap_out,
    taps,
    wz,
    head_v,
    acc,
    c_out,
    c_in,
    r_out,
    r_in,
    r_own,
    joined,
    logits,
    squares,
    stat_a,
    stat_b,
    send_sem,
    recv_sem,
    local_sem,
):
    dp = lax.axis_index("dp")
    t = lax.axis_index("tensor")
    z, xh, y = dp // 8, lax.rem(dp // 4, 2), lax.rem(dp, 4)
    xl, c = t // 2, lax.rem(t, 2)

    def device(zz, hh, yy, ll, cc):
        return (zz * 8 + hh * 4 + yy, ll * 2 + cc)

    def zo(d):
        return lax.rem(z + d, 4)

    def yo(d):
        return lax.rem(y + d, 4)

    sibling = device(z, xh, y, xl, 1 - c)
    pair = device(z, xh, y, 1 - xl, c)
    across = device(z, 1 - xh, y, xl, c)
    y_peer = [None] + [device(z, xh, yo(d), xl, c) for d in (1, 2, 3)]
    z_peer = [None] + [device(zo(d), xh, y, xl, c) for d in (1, 2, 3)]
    far_peer = [across] + [device(z, 1 - xh, yo(d), xl, c) for d in (1, 2, 3)]

    barrier = pltpu.get_barrier_semaphore()
    pair_z_peer = [pair] + [device(zo(d), xh, y, 1 - xl, c) for d in (1, 2, 3)]
    peers = [sibling] + y_peer[1:] + z_peer[1:] + far_peer + pair_z_peer
    for peer in peers:
        pl.semaphore_signal(barrier, inc=1, device_id=peer, device_id_type=pl.DeviceIdType.MESH)

    local = []

    def fetch(src, dst):
        copy = pltpu.make_async_copy(src, dst, local_sem.at[len(local)])
        copy.start()
        local.append(copy)
        return copy

    part_copy = [fetch(partial.at[k], part_v.at[k]) for k in range(3)]
    res_copy = fetch(residual, res_v)
    wz_copy = fetch(weight.at[:, pl.ds(pl.multiple_of(z * 512, 512), 512), :], wz.at[:, z])
    pl.semaphore_wait(barrier, len(peers))

    sent = []

    def make(src, dst, number, peer):
        return pltpu.make_async_remote_copy(
            src_ref=src,
            dst_ref=dst,
            send_sem=send_sem.at[number],
            recv_sem=recv_sem.at[number],
            device_id=peer,
            device_id_type=pl.DeviceIdType.MESH,
        )

    counter = iter(range(COPIES))

    def send(src, dst, peer, number=None):
        number = next(counter) if number is None else number
        copy = make(src, dst, number, peer)
        copy.start()
        sent.append(copy)
        return number

    def arrive(dst, number, peer):
        make(dst, dst, number, peer).wait_recv()

    sib_n = []
    for k in range(3):
        row = []
        for l in range(2):
            cols = pl.ds(pl.multiple_of((l * 2 + 1 - c) * 2048, 2048), 2048)
            row.append(send(partial.at[k, :, cols], sib_in.at[k, l], sibling))
        sib_n.append(row)
    wz_n = {}

    swaps = [(0, 0, 4), (1, 0, 1), (1, 1, 1), (1, 2, 2), (2, 0, 4)]

    def swap(n):
        k, first, count = swaps[n]
        for d in (1, 2, 3):
            rows = pl.ds(pl.multiple_of(zo(d) * 512 + first * 128, 128), count * 128)
            landing = pl.ds(first * 128, count * 128)
            wz_n[n, d] = send(weight.at[k, rows, :], wz.at[k, z, landing], z_peer[d])

    swap(0)
    head_copy = fetch(head, head_v)

    own_cols = pl.ds(pl.multiple_of(t * 2048, 2048), 2048)
    pair_cols = pl.ds(pl.multiple_of(((1 - xl) * 2 + c) * 2048, 2048), 2048)
    pair_n = []
    for k in range(3):
        part_copy[k].wait()
        arrive(sib_in.at[k, 0], sib_n[k][0], sibling)
        arrive(sib_in.at[k, 1], sib_n[k][1], sibling)
        pair_out[k] = (part_v[k, :, pair_cols].astype(F32) + sib_in[k, 1 - xl].astype(F32)).astype(BF16)
        pair_n.append(send(pair_out.at[k], pair_in.at[k], pair))
    res_copy.wait()
    tap_n = {}
    far_n = {}
    ring_n = {}
    half_n = {}

    def make_taps(k):
        arrive(pair_in.at[k], pair_n[k], pair)
        tap = (
            res_v[k].astype(F32)
            + (part_v[k, :, own_cols].astype(F32) + sib_in[k, xl].astype(F32))
            + pair_in[k].astype(F32)
        ).astype(BF16)
        for q in range(4):
            tap_out[k, q] = tap[:, q * 512 : (q + 1) * 512]
        for d in (1, 2, 3):
            tap_n[k, d] = send(tap_out.at[k, zo(d)], taps.at[k, y, xh, z], z_peer[d])
        taps[k, y, xh, z] = tap_out[k, z]

    def gather(k):
        for d in (1, 2, 3):
            arrive(taps.at[k, y, xh, zo(4 - d)], tap_n[k, d], z_peer[4 - d])
        block = taps.at[k, y, xh]
        far_n[k] = send(block, block, across)
        ring_n[k, 0] = [send(block, block, y_peer[1]), send(block, block, y_peer[3])]

    def gather_far(k):
        arrive(taps.at[k, y, 1 - xh], far_n[k], across)
        block = taps.at[k, y, 1 - xh]
        ring_n[k, 1] = [send(block, block, y_peer[1]), send(block, block, y_peer[3])]

    def pass_on(k, h):
        hh = 1 - xh if h else xh
        arrive(taps.at[k, yo(3), hh], ring_n[k, h][0], y_peer[3])
        low = taps.at[k, yo(3), hh, pl.ds(0, 2)]
        first = send(low, low, y_peer[1])
        arrive(taps.at[k, yo(1), hh], ring_n[k, h][1], y_peer[1])
        high = taps.at[k, yo(1), hh, pl.ds(2, 2)]
        half_n[k, h] = [first, send(high, high, y_peer[3])]

    make_taps(0)
    swap(1)
    make_taps(1)
    swap(2)
    gather(0)
    make_taps(2)
    swap(3)
    swap(4)
    gather(1)
    gather_far(0)
    gather(2)
    gather_far(1)
    gather_far(2)

    chunk_y = [y, yo(3), yo(1), yo(2)]
    c_n, r_n = {}, {}

    def multiply(j):
        slot = j % 2
        row = chunk_y[j]

        @pl.loop(0, 4)
        def _(q):
            total = jnp.zeros((512, 256), F32)
            for k in range(3):
                total += jnp.dot(taps[k, row].reshape(512, 512), wz[k, q], preferred_element_type=F32)
            acc[slot, q] = total.reshape(2, 4, 64, 256)
            for l in range(2):
                c_out[j, q, :, l] = acc[slot, q, :, l * 2 + 1 - c].astype(BF16)

        c_n[j] = send(c_out.at[j], c_in.at[j], sibling)

    ways = [(l, d) for l in range(2) for d in range(4) if l or d]

    def over_core(j):
        slot = j % 2
        arrive(c_in.at[j], c_n[j], sibling)

        @pl.loop(0, 4)
        def _(q):
            for l in range(2):
                value = acc[slot, q, :, l * 2 + c] + c_in[j, q, :, l].astype(F32)
                r_out[j, l, q] = value.astype(BF16)

        for i, (l, d) in enumerate(ways):
            peer = pair_z_peer[d] if l else z_peer[d]
            ll = 1 - xl if l else xl
            r_n[j, i] = send(r_out.at[j, ll, zo(d)], r_in.at[j, i], peer)
        r_own[j] = acc[slot, z, :, t] + c_in[j, z, :, xl].astype(F32)

    def reduce(j):
        total = r_own[j]
        for i, (l, d) in enumerate(ways):
            arrive(r_in.at[j, i], r_n[j, i], pair_z_peer[(4 - d) % 4] if l else z_peer[4 - d])
            total = total + r_in[j, i].astype(F32)
        joined[z, xh, y, j] = total.astype(BF16)

    def last_taps():
        for h in range(2):
            hh = xh if h == 0 else 1 - xh
            for k in range(3):
                arrive(taps.at[k, yo(2), hh, pl.ds(0, 2)], half_n[k, h][0], y_peer[3])
                arrive(taps.at[k, yo(2), hh, pl.ds(2, 2)], half_n[k, h][1], y_peer[1])

    group = [pl.ds(j, 1) for j in range(4)]
    spans = [pl.ds(0, 1), pl.ds(1, 2), pl.ds(3, 1)]
    one = [y_peer, z_peer]
    two = [z_peer, y_peer]
    g_far, g_ring, g_half, g_two, g_last = {}, {}, {}, {}, {}

    def place(g, h, a, b, ss=None, part=None):
        zz, yy = (zo(b), yo(a)) if h == 0 else (zo(a), yo(b))
        sl = slice(None) if ss is None else ss
        rows = slice(None) if part is None else pl.ds(part * 32, 32)
        return joined.at[zz, sl, yy, group[g], h, rows]

    def start_one(g, s):
        ss = xh if s == 0 else 1 - xh
        for h in range(2):
            block = place(g, h, 0, 0, ss)
            g_ring[g, h, s] = [send(block, block, one[h][1]), send(block, block, one[h][3])]

    def start_two(g, h, a):
        block = place(g, h, a, 0)
        g_two[g, h, a] = [send(block, block, two[h][1]), send(block, block, two[h][3])]

    def p_start(g):
        mine = joined.at[z, xh, y, group[g]]
        g_far[g] = send(mine, mine, across)
        start_one(g, 0)

    def p_far(g):
        arrive(joined.at[z, 1 - xh, y, group[g]], g_far[g], across)
        start_one(g, 1)
        for h in range(2):
            start_two(g, h, 0)

    def p_one(g):
        for s in range(2):
            ss = xh if s == 0 else 1 - xh
            for h in range(2):
                arrive(place(g, h, 3, 0, ss), g_ring[g, h, s][0], one[h][3])
                low = place(g, h, 3, 0, ss, 0)
                first = send(low, low, one[h][1])
                arrive(place(g, h, 1, 0, ss), g_ring[g, h, s][1], one[h][1])
                high = place(g, h, 1, 0, ss, 1)
                g_half[g, h, s] = [first, send(high, high, one[h][3])]
        for h in range(2):
            start_two(g, h, 3)
            start_two(g, h, 1)

    def p_one_far(g):
        for h in range(2):
            for s in range(2):
                ss = xh if s == 0 else 1 - xh
                arrive(place(g, h, 2, 0, ss, 0), g_half[g, h, s][0], one[h][3])
                arrive(place(g, h, 2, 0, ss, 1), g_half[g, h, s][1], one[h][1])
            start_two(g, h, 2)

    def p_two(g, a):
        for h in range(2):
            arrive(place(g, h, a, 3), g_two[g, h, a][0], two[h][3])
            low = place(g, h, a, 3, None, 0)
            first = send(low, low, two[h][1])
            arrive(place(g, h, a, 1), g_two[g, h, a][1], two[h][1])
            high = place(g, h, a, 1, None, 1)
            g_last[g, h, a] = [first, send(high, high, two[h][3])]

    def p_end(g):
        for h in range(2):
            for a in (0, 3, 1, 2):
                arrive(place(g, h, a, 2, None, 0), g_last[g, h, a][0], two[h][3])
                arrive(place(g, h, a, 2, None, 1), g_last[g, h, a][1], two[h][1])

    offsets = (0, 3, 1, 2)
    chunks = [(0,), (1, 2), (3,)]

    def score(g, first, count):
        n = len(chunks[g])

        @pl.loop(first, first + count)
        def _(yy):
            product = jnp.zeros((960, n * 128), F32)
            square = jnp.zeros((n * 128, 128), F32)
            for i in range(8):
                block = joined[i // 2, i % 2, yy, spans[g]].reshape(n * 128, 256)
                cols = pl.ds(pl.multiple_of((i * 4 + yy) * 256, 256), 256)
                product += lax.dot_general(
                    head_v[:, cols], block, (((1,), (1,)), ((), ())), preferred_element_type=F32
                )
                wide = block.astype(F32)
                left, right = wide[:, :128], wide[:, 128:]
                square += left * left + right * right
            for p, j in enumerate(chunks[g]):
                row = lax.rem(yy + offsets[j], 4)
                logits[row] += product[:, p * 128 : (p + 1) * 128]
                squares[row] += square[p * 128 : (p + 1) * 128]

    logits[...] = jnp.zeros_like(logits)
    squares[...] = jnp.zeros_like(squares)
    wz_copy.wait()
    for d in (1, 2, 3):
        for n, (k, first, count) in enumerate(swaps):
            arrive(wz.at[k, zo(4 - d), pl.ds(first * 128, count * 128)], wz_n[n, d], z_peer[4 - d])
    multiply(0)
    over_core(0)
    for h in range(2):
        for k in range(3):
            pass_on(k, h)
    multiply(1)
    over_core(1)
    reduce(0)
    p_start(0)
    multiply(2)
    p_far(0)
    over_core(2)
    p_one(0)
    reduce(1)
    p_start(1)
    reduce(2)
    p_start(2)
    p_far(1)
    p_one_far(0)
    p_two(0, 0)
    last_taps()
    multiply(3)
    p_far(2)
    p_one(1)
    over_core(3)
    p_two(0, 3)
    p_two(0, 1)
    p_two(0, 2)
    p_one(2)
    p_one_far(1)
    p_two(1, 0)
    reduce(3)
    p_start(3)
    p_one_far(2)
    p_two(2, 0)
    p_two(1, 3)
    p_two(1, 1)
    p_far(3)
    p_two(2, 3)
    p_two(2, 1)
    p_one(3)
    p_two(1, 2)
    head_copy.wait()
    p_end(0)
    score(0, 0, 2)
    p_two(2, 2)
    p_one_far(3)
    p_two(3, 0)
    score(0, 2, 2)
    p_two(3, 3)
    p_two(3, 1)
    p_two(3, 2)
    p_end(1)
    p_end(2)
    score(1, 0, 4)
    p_end(3)
    score(2, 0, 4)

    offset = dp * 960
    column = lax.broadcasted_iota(jnp.int32, (960, 128), 0) + offset
    every = []
    for row in range(4):
        mean = jnp.sum(squares[row].T, axis=0, keepdims=True) / D
        scaled = logits[row] / jnp.sqrt(mean + EPS)
        every.append(jnp.sum(jnp.exp(scaled), axis=0, keepdims=True))
        for s in range(3):
            low = ids[s : s + 1, row * 64 : row * 64 + 64]
            high = ids[s : s + 1, 256 + row * 64 : 256 + row * 64 + 64]
            wanted = jnp.concatenate([low, high], axis=1)
            every.append(jnp.sum(jnp.where(column == wanted, scaled, 0.0), axis=0, keepdims=True))
    stat_a[0] = jnp.concatenate(every, axis=0)
    a_n = [None] + [send(stat_a.at[0], stat_a.at[d], z_peer[d]) for d in (1, 2, 3)]
    total = stat_a[0]
    for d in (1, 2, 3):
        arrive(stat_a.at[d], a_n[d], z_peer[4 - d])
        total = total + stat_a[d]
    stat_b[0, 0] = total
    b_n = {}
    for s in range(2):
        for d in range(4):
            if s or d:
                peer = far_peer[d] if s else y_peer[d]
                b_n[s, d] = send(stat_b.at[0, 0], stat_b.at[s, d], peer)
    for s in range(2):
        for d in range(4):
            if s or d:
                peer = far_peer[(4 - d) % 4] if s else y_peer[4 - d]
                arrive(stat_b.at[s, d], b_n[s, d], peer)
                total = total + stat_b[s, d]
    loss = [jnp.log(total[row * 4 : row * 4 + 1]) - total[row * 4 + 1 : row * 4 + 4] for row in range(4)]
    losses[...] = jnp.concatenate([v[:, :64] for v in loss] + [v[:, 64:] for v in loss], axis=1)
    for copy in sent:
        copy.wait_send()


def shards(residual, partials, join_weight, head_weight, target_ids):
    vmem = pl.BlockSpec(memory_space=pltpu.VMEM)
    hbm = pl.BlockSpec(memory_space=pl.ANY)
    return pl.pallas_call(
        kernel,
        out_shape=jax.ShapeDtypeStruct((3, 512), F32),
        in_specs=[hbm, hbm, hbm, hbm, vmem],
        out_specs=vmem,
        scratch_shapes=[
            pltpu.VMEM((3, 64, 8192), BF16),
            pltpu.VMEM((3, 64, 2048), BF16),
            pltpu.VMEM((3, 2, 64, 2048), BF16),
            pltpu.VMEM((3, 64, 2048), BF16),
            pltpu.VMEM((3, 64, 2048), BF16),
            pltpu.VMEM((3, 4, 64, 512), BF16),
            pltpu.VMEM((3, 4, 2, 4, 64, 512), BF16),
            pltpu.VMEM((3, 4, 512, 256), BF16),
            pltpu.VMEM((960, 8192), BF16),
            pltpu.VMEM((2, 4, 2, 4, 64, 256), F32),
            pltpu.VMEM((4, 4, 2, 2, 64, 256), BF16),
            pltpu.VMEM((4, 4, 2, 2, 64, 256), BF16),
            pltpu.VMEM((4, 2, 4, 2, 64, 256), BF16),
            pltpu.VMEM((4, 7, 2, 64, 256), BF16),
            pltpu.VMEM((4, 2, 64, 256), F32),
            pltpu.VMEM((4, 2, 4, 4, 2, 64, 256), BF16),
            pltpu.VMEM((4, 960, 128), F32),
            pltpu.VMEM((4, 128, 128), F32),
            pltpu.VMEM((4, 16, 128), F32),
            pltpu.VMEM((2, 4, 16, 128), F32),
            pltpu.SemaphoreType.DMA((COPIES,)),
            pltpu.SemaphoreType.DMA((COPIES,)),
            pltpu.SemaphoreType.DMA((8,)),
        ],
        compiler_params=pltpu.CompilerParams(
            collective_id=0, has_side_effects=True, vmem_limit_bytes=63 * 1024 * 1024
        ),
    )(residual, partials.reshape(3, 64, 8192), join_weight, head_weight.T, target_ids)


def solution(mesh):
    placed = (
        P(None, "dp", "tensor"),
        P(None, "dp", "tensor", None),
        P(None, "tensor", "dp"),
        P(None, "dp"),
        P(None, "tensor"),
    )
    return jax.shard_map(
        shards, mesh=mesh, in_specs=placed, out_specs=P(None, "tensor"), check_vma=False
    )
```

```python
import jax
import jax.numpy as jnp
from jax import lax
from jax.experimental import pallas as pl
from jax.experimental.pallas import tpu as pltpu
from jax.sharding import PartitionSpec as P

D = 8192
EPS = 1e-05
F32 = jnp.float32
BF16 = jnp.bfloat16
COPIES = 360


def kernel(
    residual,
    partial,
    weight,
    head,
    ids,
    losses,
    part_v,
    res_v,
    sib_in,
    pair_out,
    pair_in,
    tap_out,
    taps,
    wz,
    head_v,
    acc,
    c_out,
    c_in,
    r_out,
    r_in,
    r_own,
    joined,
    logits,
    squares,
    stat_a,
    stat_b,
    send_sem,
    recv_sem,
    local_sem,
):
    dp = lax.axis_index("dp")
    t = lax.axis_index("tensor")
    z, xh, y = dp // 8, lax.rem(dp // 4, 2), lax.rem(dp, 4)
    xl, c = t // 2, lax.rem(t, 2)

    def device(zz, hh, yy, ll, cc):
        return (zz * 8 + hh * 4 + yy, ll * 2 + cc)

    def zo(d):
        return lax.rem(z + d, 4)

    def yo(d):
        return lax.rem(y + d, 4)

    sibling = device(z, xh, y, xl, 1 - c)
    pair = device(z, xh, y, 1 - xl, c)
    across = device(z, 1 - xh, y, xl, c)
    y_peer = [None] + [device(z, xh, yo(d), xl, c) for d in (1, 2, 3)]
    z_peer = [None] + [device(zo(d), xh, y, xl, c) for d in (1, 2, 3)]
    far_peer = [across] + [device(z, 1 - xh, yo(d), xl, c) for d in (1, 2, 3)]

    barrier = pltpu.get_barrier_semaphore()
    pair_z_peer = [pair] + [device(zo(d), xh, y, 1 - xl, c) for d in (1, 2, 3)]
    peers = [sibling] + y_peer[1:] + z_peer[1:] + far_peer + pair_z_peer
    for peer in peers:
        pl.semaphore_signal(barrier, inc=1, device_id=peer, device_id_type=pl.DeviceIdType.MESH)

    local = []

    def fetch(src, dst):
        copy = pltpu.make_async_copy(src, dst, local_sem.at[len(local)])
        copy.start()
        local.append(copy)
        return copy

    part_copy = [fetch(partial.at[k], part_v.at[k]) for k in range(3)]
    res_copy = fetch(residual, res_v)
    wz_copy = fetch(weight.at[:, pl.ds(pl.multiple_of(z * 512, 512), 512), :], wz.at[:, z])
    pl.semaphore_wait(barrier, len(peers))

    sent = []

    def make(src, dst, number, peer):
        return pltpu.make_async_remote_copy(
            src_ref=src,
            dst_ref=dst,
            send_sem=send_sem.at[number],
            recv_sem=recv_sem.at[number],
            device_id=peer,
            device_id_type=pl.DeviceIdType.MESH,
        )

    counter = iter(range(COPIES))

    def send(src, dst, peer, number=None):
        number = next(counter) if number is None else number
        copy = make(src, dst, number, peer)
        copy.start()
        sent.append(copy)
        return number

    def arrive(dst, number, peer):
        make(dst, dst, number, peer).wait_recv()

    sib_n = []
    for k in range(3):
        row = []
        for l in range(2):
            cols = pl.ds(pl.multiple_of((l * 2 + 1 - c) * 2048, 2048), 2048)
            row.append(send(partial.at[k, :, cols], sib_in.at[k, l], sibling))
        sib_n.append(row)
    wz_n = {}

    swaps = [(0, 0, 4), (1, 0, 1), (1, 1, 1), (1, 2, 2), (2, 0, 4)]

    def swap(n):
        k, first, count = swaps[n]
        for d in (1, 2, 3):
            rows = pl.ds(pl.multiple_of(zo(d) * 512 + first * 128, 128), count * 128)
            landing = pl.ds(first * 128, count * 128)
            wz_n[n, d] = send(weight.at[k, rows, :], wz.at[k, z, landing], z_peer[d])

    swap(0)
    head_copy = fetch(head, head_v)

    own_cols = pl.ds(pl.multiple_of(t * 2048, 2048), 2048)
    pair_cols = pl.ds(pl.multiple_of(((1 - xl) * 2 + c) * 2048, 2048), 2048)
    pieces = [(0, 0, 32), (0, 32, 32), (1, 0, 64), (2, 0, 64)]
    pair_n, tap_n, far_n, ring_n, half_n = {}, {}, {}, {}, {}

    def block_of(p, yy, hh, zz=slice(None)):
        k, first, count = pieces[p]
        return taps.at[k, yy, hh, zz, pl.ds(first, count)]

    def send_pair(p):
        k, first, count = pieces[p]
        rows = pl.ds(first, count)
        if first == 0:
            part_copy[k].wait()
            arrive(sib_in.at[k, 0], sib_n[k][0], sibling)
            arrive(sib_in.at[k, 1], sib_n[k][1], sibling)
        pair_out[k, rows] = (
            part_v[k, rows, pair_cols].astype(F32) + sib_in[k, 1 - xl, rows].astype(F32)
        ).astype(BF16)
        pair_n[p] = send(pair_out.at[k, rows], pair_in.at[k, rows], pair)

    def make_taps(p):
        k, first, count = pieces[p]
        rows = pl.ds(first, count)
        arrive(pair_in.at[k, rows], pair_n[p], pair)
        tap = (
            res_v[k, rows].astype(F32)
            + (part_v[k, rows, own_cols].astype(F32) + sib_in[k, xl, rows].astype(F32))
            + pair_in[k, rows].astype(F32)
        ).astype(BF16)
        for q in range(4):
            tap_out[k, q, rows] = tap[:, q * 512 : (q + 1) * 512]
        for d in (1, 2, 3):
            tap_n[p, d] = send(tap_out.at[k, zo(d), rows], block_of(p, y, xh, z), z_peer[d])
        taps[k, y, xh, z, rows] = tap_out[k, z, rows]

    def gather(p):
        for d in (1, 2, 3):
            arrive(block_of(p, y, xh, zo(4 - d)), tap_n[p, d], z_peer[4 - d])
        block = block_of(p, y, xh)
        far_n[p] = send(block, block, across)
        ring_n[p, 0] = [send(block, block, y_peer[1]), send(block, block, y_peer[3])]

    def gather_far(p):
        block = block_of(p, y, 1 - xh)
        arrive(block, far_n[p], across)
        ring_n[p, 1] = [send(block, block, y_peer[1]), send(block, block, y_peer[3])]

    def pass_on(p, h):
        hh = 1 - xh if h else xh
        arrive(block_of(p, yo(3), hh), ring_n[p, h][0], y_peer[3])
        low = block_of(p, yo(3), hh, pl.ds(0, 2))
        first = send(low, low, y_peer[1])
        arrive(block_of(p, yo(1), hh), ring_n[p, h][1], y_peer[1])
        high = block_of(p, yo(1), hh, pl.ds(2, 2))
        half_n[p, h] = [first, send(high, high, y_peer[3])]

    for p in range(4):
        send_pair(p)
    res_copy.wait()
    make_taps(0)
    make_taps(1)
    swap(1)
    gather(0)
    make_taps(2)
    swap(2)
    gather(1)
    make_taps(3)
    gather(2)
    swap(3)
    swap(4)
    gather_far(0)
    gather_far(1)
    gather(3)
    gather_far(2)
    gather_far(3)

    chunk_y = [y, yo(3), yo(1), yo(2)]
    c_n, r_n = {}, {}

    def multiply(j):
        slot = j % 2
        row = chunk_y[j]

        @pl.loop(0, 4)
        def _(q):
            total = jnp.zeros((512, 256), F32)
            for k in range(3):
                total += jnp.dot(taps[k, row].reshape(512, 512), wz[k, q], preferred_element_type=F32)
            acc[slot, q] = total.reshape(2, 4, 64, 256)
            for l in range(2):
                c_out[j, q, :, l] = acc[slot, q, :, l * 2 + 1 - c].astype(BF16)

        c_n[j] = send(c_out.at[j], c_in.at[j], sibling)

    ways = [(l, d) for l in range(2) for d in range(4) if l or d]

    def over_core(j):
        slot = j % 2
        arrive(c_in.at[j], c_n[j], sibling)

        @pl.loop(0, 4)
        def _(q):
            for l in range(2):
                value = acc[slot, q, :, l * 2 + c] + c_in[j, q, :, l].astype(F32)
                r_out[j, l, q] = value.astype(BF16)

        for i, (l, d) in enumerate(ways):
            peer = pair_z_peer[d] if l else z_peer[d]
            ll = 1 - xl if l else xl
            r_n[j, i] = send(r_out.at[j, ll, zo(d)], r_in.at[j, i], peer)
        r_own[j] = acc[slot, z, :, t] + c_in[j, z, :, xl].astype(F32)

    def reduce(j):
        total = r_own[j]
        for i, (l, d) in enumerate(ways):
            arrive(r_in.at[j, i], r_n[j, i], pair_z_peer[(4 - d) % 4] if l else z_peer[4 - d])
            total = total + r_in[j, i].astype(F32)
        joined[z, xh, y, j] = total.astype(BF16)

    def last_taps():
        for h in range(2):
            hh = xh if h == 0 else 1 - xh
            for p in range(4):
                arrive(block_of(p, yo(2), hh, pl.ds(0, 2)), half_n[p, h][0], y_peer[3])
                arrive(block_of(p, yo(2), hh, pl.ds(2, 2)), half_n[p, h][1], y_peer[1])

    group = [pl.ds(j, 1) for j in range(4)]
    spans = [pl.ds(0, 1), pl.ds(1, 2), pl.ds(3, 1)]
    one = [y_peer, z_peer]
    two = [z_peer, y_peer]
    g_far, g_ring, g_half, g_two, g_last = {}, {}, {}, {}, {}

    def place(g, h, a, b, ss=None, part=None):
        zz, yy = (zo(b), yo(a)) if h == 0 else (zo(a), yo(b))
        sl = slice(None) if ss is None else ss
        rows = slice(None) if part is None else pl.ds(part * 32, 32)
        return joined.at[zz, sl, yy, group[g], h, rows]

    def start_one(g, s):
        ss = xh if s == 0 else 1 - xh
        for h in range(2):
            block = place(g, h, 0, 0, ss)
            g_ring[g, h, s] = [send(block, block, one[h][1]), send(block, block, one[h][3])]

    def start_two(g, h, a):
        block = place(g, h, a, 0)
        g_two[g, h, a] = [send(block, block, two[h][1]), send(block, block, two[h][3])]

    def p_start(g):
        mine = joined.at[z, xh, y, group[g]]
        g_far[g] = send(mine, mine, across)
        start_one(g, 0)

    def p_far(g):
        arrive(joined.at[z, 1 - xh, y, group[g]], g_far[g], across)
        start_one(g, 1)
        for h in range(2):
            start_two(g, h, 0)

    def p_one(g):
        for s in range(2):
            ss = xh if s == 0 else 1 - xh
            for h in range(2):
                arrive(place(g, h, 3, 0, ss), g_ring[g, h, s][0], one[h][3])
                low = place(g, h, 3, 0, ss, 0)
                first = send(low, low, one[h][1])
                arrive(place(g, h, 1, 0, ss), g_ring[g, h, s][1], one[h][1])
                high = place(g, h, 1, 0, ss, 1)
                g_half[g, h, s] = [first, send(high, high, one[h][3])]
        for h in range(2):
            start_two(g, h, 3)
            start_two(g, h, 1)

    def p_one_far(g):
        for h in range(2):
            for s in range(2):
                ss = xh if s == 0 else 1 - xh
                arrive(place(g, h, 2, 0, ss, 0), g_half[g, h, s][0], one[h][3])
                arrive(place(g, h, 2, 0, ss, 1), g_half[g, h, s][1], one[h][1])
            start_two(g, h, 2)

    def p_two(g, a):
        for h in range(2):
            arrive(place(g, h, a, 3), g_two[g, h, a][0], two[h][3])
            low = place(g, h, a, 3, None, 0)
            first = send(low, low, two[h][1])
            arrive(place(g, h, a, 1), g_two[g, h, a][1], two[h][1])
            high = place(g, h, a, 1, None, 1)
            g_last[g, h, a] = [first, send(high, high, two[h][3])]

    def p_end(g):
        for h in range(2):
            for a in (0, 3, 1, 2):
                arrive(place(g, h, a, 2, None, 0), g_last[g, h, a][0], two[h][3])
                arrive(place(g, h, a, 2, None, 1), g_last[g, h, a][1], two[h][1])

    offsets = (0, 3, 1, 2)
    chunks = [(0,), (1, 2), (3,)]

    def score(g, first, count):
        n = len(chunks[g])

        @pl.loop(first, first + count)
        def _(yy):
            product = jnp.zeros((960, n * 128), F32)
            square = jnp.zeros((n * 128, 128), F32)
            for i in range(8):
                block = joined[i // 2, i % 2, yy, spans[g]].reshape(n * 128, 256)
                cols = pl.ds(pl.multiple_of((i * 4 + yy) * 256, 256), 256)
                product += lax.dot_general(
                    head_v[:, cols], block, (((1,), (1,)), ((), ())), preferred_element_type=F32
                )
                wide = block.astype(F32)
                left, right = wide[:, :128], wide[:, 128:]
                square += left * left + right * right
            for p, j in enumerate(chunks[g]):
                row = lax.rem(yy + offsets[j], 4)
                logits[row] += product[:, p * 128 : (p + 1) * 128]
                squares[row] += square[p * 128 : (p + 1) * 128]

    logits[...] = jnp.zeros_like(logits)
    squares[...] = jnp.zeros_like(squares)
    wz_copy.wait()
    for d in (1, 2, 3):
        for n, (k, first, count) in enumerate(swaps):
            arrive(wz.at[k, zo(4 - d), pl.ds(first * 128, count * 128)], wz_n[n, d], z_peer[4 - d])
    multiply(0)
    over_core(0)
    for h in range(2):
        for p in range(4):
            pass_on(p, h)
    multiply(1)
    reduce(0)
    p_start(0)
    over_core(1)
    multiply(2)
    p_far(0)
    over_core(2)
    p_one(0)
    reduce(1)
    p_start(1)
    p_one_far(0)
    p_two(0, 0)
    reduce(2)
    p_start(2)
    p_far(1)
    last_taps()
    multiply(3)
    p_far(2)
    p_one(1)
    over_core(3)
    p_two(0, 3)
    p_two(0, 1)
    p_two(0, 2)
    p_one(2)
    p_one_far(1)
    p_two(1, 0)
    reduce(3)
    p_start(3)
    p_one_far(2)
    p_two(2, 0)
    p_two(1, 3)
    p_two(1, 1)
    p_far(3)
    p_two(2, 3)
    p_two(2, 1)
    p_one(3)
    p_two(1, 2)
    head_copy.wait()
    p_end(0)
    score(0, 0, 2)
    p_two(2, 2)
    p_one_far(3)
    p_two(3, 0)
    score(0, 2, 2)
    p_two(3, 3)
    p_two(3, 1)
    p_two(3, 2)
    p_end(1)
    p_end(2)
    score(1, 0, 4)
    p_end(3)
    score(2, 0, 4)

    offset = dp * 960
    column = lax.broadcasted_iota(jnp.int32, (960, 128), 0) + offset
    every = []
    for row in range(4):
        mean = jnp.sum(squares[row].T, axis=0, keepdims=True) / D
        scaled = logits[row] / jnp.sqrt(mean + EPS)
        every.append(jnp.sum(jnp.exp(scaled), axis=0, keepdims=True))
        for s in range(3):
            low = ids[s : s + 1, row * 64 : row * 64 + 64]
            high = ids[s : s + 1, 256 + row * 64 : 256 + row * 64 + 64]
            wanted = jnp.concatenate([low, high], axis=1)
            every.append(jnp.sum(jnp.where(column == wanted, scaled, 0.0), axis=0, keepdims=True))
    stat_a[0] = jnp.concatenate(every, axis=0)
    a_n = [None] + [send(stat_a.at[0], stat_a.at[d], z_peer[d]) for d in (1, 2, 3)]
    total = stat_a[0]
    for d in (1, 2, 3):
        arrive(stat_a.at[d], a_n[d], z_peer[4 - d])
        total = total + stat_a[d]
    stat_b[0, 0] = total
    b_n = {}
    for s in range(2):
        for d in range(4):
            if s or d:
                peer = far_peer[d] if s else y_peer[d]
                b_n[s, d] = send(stat_b.at[0, 0], stat_b.at[s, d], peer)
    for s in range(2):
        for d in range(4):
            if s or d:
                peer = far_peer[(4 - d) % 4] if s else y_peer[4 - d]
                arrive(stat_b.at[s, d], b_n[s, d], peer)
                total = total + stat_b[s, d]
    loss = [jnp.log(total[row * 4 : row * 4 + 1]) - total[row * 4 + 1 : row * 4 + 4] for row in range(4)]
    losses[...] = jnp.concatenate([v[:, :64] for v in loss] + [v[:, 64:] for v in loss], axis=1)
    for copy in sent:
        copy.wait_send()


def shards(residual, partials, join_weight, head_weight, target_ids):
    vmem = pl.BlockSpec(memory_space=pltpu.VMEM)
    hbm = pl.BlockSpec(memory_space=pl.ANY)
    return pl.pallas_call(
        kernel,
        out_shape=jax.ShapeDtypeStruct((3, 512), F32),
        in_specs=[hbm, hbm, hbm, hbm, vmem],
        out_specs=vmem,
        scratch_shapes=[
            pltpu.VMEM((3, 64, 8192), BF16),
            pltpu.VMEM((3, 64, 2048), BF16),
            pltpu.VMEM((3, 2, 64, 2048), BF16),
            pltpu.VMEM((3, 64, 2048), BF16),
            pltpu.VMEM((3, 64, 2048), BF16),
            pltpu.VMEM((3, 4, 64, 512), BF16),
            pltpu.VMEM((3, 4, 2, 4, 64, 512), BF16),
            pltpu.VMEM((3, 4, 512, 256), BF16),
            pltpu.VMEM((960, 8192), BF16),
            pltpu.VMEM((2, 4, 2, 4, 64, 256), F32),
            pltpu.VMEM((4, 4, 2, 2, 64, 256), BF16),
            pltpu.VMEM((4, 4, 2, 2, 64, 256), BF16),
            pltpu.VMEM((4, 2, 4, 2, 64, 256), BF16),
            pltpu.VMEM((4, 7, 2, 64, 256), BF16),
            pltpu.VMEM((4, 2, 64, 256), F32),
            pltpu.VMEM((4, 2, 4, 4, 2, 64, 256), BF16),
            pltpu.VMEM((4, 960, 128), F32),
            pltpu.VMEM((4, 128, 128), F32),
            pltpu.VMEM((4, 16, 128), F32),
            pltpu.VMEM((2, 4, 16, 128), F32),
            pltpu.SemaphoreType.DMA((COPIES,)),
            pltpu.SemaphoreType.DMA((COPIES,)),
            pltpu.SemaphoreType.DMA((8,)),
        ],
        compiler_params=pltpu.CompilerParams(
            collective_id=0, has_side_effects=True, vmem_limit_bytes=63 * 1024 * 1024
        ),
    )(residual, partials.reshape(3, 64, 8192), join_weight, head_weight.T, target_ids)


def solution(mesh):
    placed = (
        P(None, "dp", "tensor"),
        P(None, "dp", "tensor", None),
        P(None, "tensor", "dp"),
        P(None, "dp"),
        P(None, "tensor"),
    )
    return jax.shard_map(
        shards, mesh=mesh, in_specs=placed, out_specs=P(None, "tensor"), check_vma=False
    )
```
